512 devices in a mesh: row: 16 (over z_lo, x, core), col: 32 (over z_hi, y).
Axes of the slice: x: 4, y: 8, z: 8 (z_hi: 4, z_lo: 2; z = z_hi * 2 + z_lo), core: 2. Of those that a mesh axis runs over, the one named last changes fastest.
Arguments:
- inputs: bfloat16 [256, 12288], P('col', 'row'), may hold values from -6 to 6
- weight: bfloat16 [12288, 24576], P('row', 'col'), may hold values from -0.0546875 to 0.0546875
- hidden_bias: float32 [24576], P('col'), may hold values from -3 to 3
- cotangent: bfloat16 [256, 24576], P('row', 'col'), may hold values from -6 to 6
Outputs:
- hidden: bfloat16 [256, 24576], P('row', 'col')
- grad_input: bfloat16 [256, 12288], P('col', 'row')
- grad_weight: bfloat16 [12288, 24576], P('row', 'col')
- grad_bias: float32 [24576], P('col')
The draws below stay inside these ranges and needn't reach their ends.
All inputs are finite; a program needn't handle non-finite values.
Results may differ from the reference program's by a relative error of at most 0.0049.
Values may be sent and summed in bfloat16 or wider, within the bound.
A program may use at most 64 MiB of HBM per device.

```python
import jax
import jax.numpy as jnp
from jax import lax

D = 12288
F = 24576
TOKENS = 256


def strengthened(result, rng, source, target, shards_of, factor):
    def block_of(axis_at):
        return (jnp.arange(result.shape[axis_at]) // (result.shape[axis_at] // shards_of)).reshape((-1,) + (1,) * (result.ndim - 1 - axis_at))

    near = jax.random.permutation(rng, shards_of)[block_of(target)]
    second = (block_of(target) + shards_of // 2) % shards_of
    return jnp.where((block_of(source) == near) | (block_of(source) == second), factor * result, result)


def shard_levels(own_key, extent, shards, least, top_value):
    loudness = 1.0
    for dim, parts in shards:
        draws = jax.random.uniform(jax.random.fold_in(jax.random.fold_in(own_key, 6), dim), (parts,), jnp.float32, least / len(shards), top_value / len(shards))
        loudness = loudness * jnp.repeat(jnp.exp(draws), extent[dim] // parts).reshape((-1,) + (1,) * (len(extent) - 1 - dim))
    return loudness


def centred(stream_key, extent, scale, limit, split=(), kind=jnp.bfloat16):
    level = shard_levels(stream_key, extent, split, -0.22, 0.18) if split else 1.0
    array = jax.random.normal(stream_key, extent, jnp.float32) * scale * level
    return jnp.minimum(jnp.maximum(array, -limit), limit).astype(kind)


def noise_with(own_key, dims, spread, reach, shards, heavy, kind=jnp.bfloat16):
    entries = spread * jax.random.normal(own_key, dims, jnp.float32)
    if shards:
        entries = entries * shard_levels(own_key, dims, shards, -0.22, 0.18)
    return jnp.clip(strengthened(entries, jax.random.fold_in(own_key, 3), *heavy), -reach, reach).astype(kind)


def setup_inputs(seed: int = 0) -> dict:
    streams_of = jax.random.split(jax.random.key(seed), 5)
    inputs = noise_with(streams_of[0], (TOKENS, D), 1.0, 6.0, ((0, 32), (1, 16)), (1, 0, 32, 2.75))
    weight = centred(streams_of[1], (D, F), D ** -0.5, 0.0546875, ((0, 16), (1, 32)))
    hidden_bias = centred(streams_of[2], (F,), 0.5, 3.0, ((0, 32),), jnp.float32)
    cotangent = noise_with(streams_of[3], (TOKENS, F), 1.0, 6.0, ((0, 16), (1, 32)), (1, 0, 32, 2.75))
    return dict(inputs=inputs, weight=weight, hidden_bias=hidden_bias, cotangent=cotangent)


def gelu_tanh(values):
    return jax.nn.gelu(values, approximate=True)

def gelu_pair(preact, upstream):
    output, pullback = jax.vjp(gelu_tanh, preact)
    return (output, pullback(upstream)[0])

def reference(inputs, weight, hidden_bias, cotangent):
    preact = jnp.dot(inputs, weight, preferred_element_type=jnp.float32) + hidden_bias.astype(jnp.float32)
    output, slope = gelu_pair(preact, cotangent.astype(jnp.float32))
    hidden = output.astype(jnp.bfloat16)
    grad_pre = slope.astype(jnp.bfloat16)
    grad_input = jnp.dot(grad_pre, weight.T, preferred_element_type=jnp.float32).astype(jnp.bfloat16)
    grad_weight = jnp.dot(inputs.T, grad_pre, preferred_element_type=jnp.float32).astype(jnp.bfloat16)
    grad_bias = lax.optimization_barrier(jnp.sum(grad_pre.astype(jnp.float32), axis=0))
    return (hidden, grad_input, grad_weight, grad_bias)
```

```python
import jax
import jax.numpy as jnp
from jax import lax
from jax.experimental import pallas as pl
from jax.experimental.pallas import tpu as pltpu
from jax.sharding import PartitionSpec as P

MESH = pl.DeviceIdType.MESH
CORES, XS, ZLO, YS, ZHI = 2, 4, 2, 8, 4
ROWS, COLS = ZLO * XS * CORES, ZHI * YS
BF16, F32 = jnp.bfloat16, jnp.float32

ROW_OFFSETS = [
    (dz, dx, dc)
    for dz, dx in ((1, 2), (0, 2), (1, 1), (1, 3), (0, 1), (0, 3), (1, 0), (0, 0))
    for dc in (1, 0)
    if dz or dx or dc
]
Z_ORDER = (0, 1, 3, 2)
FAR_SIDE = {0: 1, 1: -1, 3: 1, 2: -1}


def gelu_and_slope(v):
    c, a = 0.7978845608028654, 0.044715
    v2 = v * v
    t = jnp.tanh(c * (v + a * (v2 * v)))
    half = 0.5 * (1.0 + t)
    return v * half, half + (0.5 * v) * (1.0 - t * t) * (c * (1.0 + (3.0 * a) * v2))


def kernel(
    x_hbm, w_hbm, b_ref, cot_ref,
    hid_ref, gi_ref, gw_hbm, gb_ref,
    w_v, xg, xn, xt, part, psend, precv, g_v, part2, gw_v,
    raw, raw_in, mid, mid_in, zout, zin,
    local_sem, za_s, za_r, ya_s, ya_r, p_s, p_r, g_s, g_r, e_s, e_r, ez_s, ez_r,
):
    r = lax.axis_index("row")
    c = lax.axis_index("col")
    core, x, zlo = lax.rem(r, 2), lax.rem(lax.div(r, 2), XS), lax.div(r, 8)
    y, z = lax.rem(c, YS), lax.div(c, YS)

    def at_row(dz, dx, dc):
        return (lax.rem(zlo + dz, ZLO) * XS + lax.rem(x + dx, XS)) * CORES + lax.rem(core + dc, CORES)

    def wy(d):
        return lax.rem(y + (d + YS), YS)

    def wz(d):
        return lax.rem(z + (d + ZHI), ZHI)

    def to_row(o):
        return {"row": at_row(*o), "col": c}

    def to_y(d):
        return {"row": r, "col": z * YS + wy(d)}

    def to_z(d):
        return {"row": r, "col": wz(d) * YS + y}

    def send(src, dst, s, q, dev):
        return pltpu.make_async_remote_copy(
            src_ref=src, dst_ref=dst, send_sem=s, recv_sem=q, device_id=dev, device_id_type=MESH
        )

    peers = [to_y(d) for d in (1, -1, 2, -2)] + [to_z(d) for d in (1, 2, 3)] + [to_row(o) for o in ROW_OFFSETS]
    barrier = pltpu.get_barrier_semaphore()
    for dev in peers:
        pl.semaphore_signal(barrier, inc=1, device_id=dev, device_id_type=MESH)
    x_in = pltpu.make_async_copy(x_hbm, xg.at[y, z], local_sem.at[0])
    w_in = pltpu.make_async_copy(w_hbm, w_v, local_sem.at[1])
    x_in.start()
    w_in.start()
    x_in.wait()
    pl.semaphore_wait(barrier, len(peers))

    pending = []
    zc = {}
    for d in (2, 1, 3):
        zc[d] = send(xg.at[y, z], xg.at[y, z], za_s.at[d], za_r.at[d], to_z(d))
        zc[d].start()
        pending.append(zc[d])
    near = {}
    for k in Z_ORDER:
        zk = wz(-k)
        if k:
            zc[k].wait_recv()
        for i, d in enumerate((2, -2, 1, -1)):
            block = xg.at[y, zk]
            near[k, d] = send(block, block, ya_s.at[k, i], ya_r.at[k, i], to_y(d))
            near[k, d].start()
            pending.append(near[k, d])
    far = []
    for k in Z_ORDER:
        zk = wz(-k)
        for i, side in enumerate((1, -1)):
            near[k, 2 * side].wait_recv()
            block = xg.at[wy(-2 * side), zk]
            if FAR_SIDE[k] == side:
                far.append(send(block, block, ya_s.at[k, 4], ya_r.at[k, 4], to_y(2 * side)))
                far[-1].start()
            far.append(send(block, block, ya_s.at[k, 5 + i], ya_r.at[k, 5 + i], to_y(side)))
            far[-1].start()
    pending += far
    w_in.wait()
    for k in Z_ORDER:
        near[k, 1].wait_recv()
        near[k, -1].wait_recv()
    for cp in far:
        cp.wait_recv()

    for rr in range(ROWS):
        zz, yy = rr // 4, 2 * (rr % 4)
        pair = jnp.concatenate([xg[yy, zz].astype(F32), xg[yy + 1, zz].astype(F32)], axis=0)
        xn[pl.ds(16 * rr, 16), :] = pair.astype(BF16)
    part[...] = jnp.dot(xn[...], w_v[...], preferred_element_type=F32)

    sums = []
    for i, o in enumerate(ROW_OFFSETS):
        rows = pl.ds(pl.multiple_of(at_row(*o) * 16, 16), 16)
        psend[i] = part[rows, :].astype(BF16)
        sums.append(send(psend.at[i], precv.at[i], p_s.at[i], p_r.at[i], to_row(o)))
        sums[-1].start()
    pending += sums
    mine = pl.ds(pl.multiple_of(r * 16, 16), 16)
    v = part[mine, :] + b_ref[...].reshape(1, -1)
    xt[...] = xn[...].T
    for i in reversed(range(len(ROW_OFFSETS))):
        sums[i].wait_recv()
        v = v + precv[i].astype(F32)

    hidden, slope = gelu_and_slope(v)
    g_v[mine, :] = (cot_ref[...].astype(F32) * slope).astype(BF16)

    grads = []
    for i, o in enumerate(ROW_OFFSETS):
        grads.append(send(g_v.at[mine, :], g_v.at[mine, :], g_s.at[i], g_r.at[i], to_row(o)))
        grads[-1].start()
    pending += grads
    hid_ref[...] = hidden.astype(BF16)
    for cp in grads:
        cp.wait_recv()

    part2[...] = lax.dot_general(g_v[...], w_v[...], (((1,), (1,)), ((), ())), preferred_element_type=F32)

    def share(d, zk):
        return part2[pl.ds(pl.multiple_of((zk * YS + wy(d)) * 8, 8), 8), :]

    order = (2, 1, 3, 0)
    legs = {}
    for k in order:
        zk = wz(k)
        side = FAR_SIDE[k]
        for j, final, via in ((0, 4, 2 * side), (1, 3, 1), (2, -3, -1), (3, 1, 1), (4, -1, -1)):
            raw[k, j] = share(final, zk).astype(BF16)
            legs[k, j] = send(raw.at[k, j], raw_in.at[k, j], e_s.at[k, j], e_r.at[k, j], to_y(via))
            legs[k, j].start()
            pending.append(legs[k, j])

    gw_v[...] = jnp.dot(xt[...], g_v[...], preferred_element_type=F32).astype(BF16)
    gw_out = pltpu.make_async_copy(gw_v, gw_hbm, local_sem.at[0])
    gw_out.start()
    gb_ref[...] = jnp.sum(g_v[...].astype(F32), axis=0)

    for k in order:
        zk = wz(k)
        legs[k, 0].wait_recv()
        for j, side in ((0, 1), (1, -1)):
            legs[k, 1 + j].wait_recv()
            s = share(2 * side, zk) + raw_in[k, 1 + j].astype(F32)
            if FAR_SIDE[k] == side:
                s = s + raw_in[k, 0].astype(F32)
            mid[k, j] = s.astype(BF16)
            legs[k, 5 + j] = send(mid.at[k, j], mid_in.at[k, j], e_s.at[k, 5 + j], e_r.at[k, 5 + j], to_y(2 * side))
            legs[k, 5 + j].start()
            pending.append(legs[k, 5 + j])
    last = {}
    for k in order:
        zk = wz(k)
        s = share(0, zk)
        for j in (3, 4):
            legs[k, j].wait_recv()
            s = s + raw_in[k, j].astype(F32)
        for j in (0, 1):
            legs[k, 5 + j].wait_recv()
            s = s + mid_in[k, j].astype(F32)
        if k:
            zout[k] = s
            last[k] = send(zout.at[k], zin.at[k], ez_s.at[k], ez_r.at[k], to_z(k))
            last[k].start()
            pending.append(last[k])
    for k in (1, 3, 2):
        last[k].wait_recv()
        s = s + zin[k]
    gi_ref[...] = s.astype(BF16)
    for cp in pending:
        cp.wait_send()
    gw_out.wait()


def shards(inputs, weight, hidden_bias, cotangent):
    tok, feat = inputs.shape
    hid = weight.shape[1]
    all_tok = tok * COLS
    vmem = pl.BlockSpec(memory_space=pltpu.VMEM)
    hbm = pl.BlockSpec(memory_space=pl.ANY)
    dma = pltpu.SemaphoreType.DMA
    n_row = len(ROW_OFFSETS)
    return pl.pallas_call(
        kernel,
        out_shape=(
            jax.ShapeDtypeStruct(cotangent.shape, BF16),
            jax.ShapeDtypeStruct(inputs.shape, BF16),
            jax.ShapeDtypeStruct(weight.shape, BF16),
            jax.ShapeDtypeStruct(hidden_bias.shape, F32),
        ),
        in_specs=[hbm, hbm, vmem, vmem],
        out_specs=(vmem, vmem, hbm, vmem),
        scratch_shapes=[
            pltpu.VMEM((feat, hid), BF16),
            pltpu.VMEM((YS, ZHI, tok, feat), BF16),
            pltpu.VMEM((all_tok, feat), BF16),
            pltpu.VMEM((feat, all_tok), BF16),
            pltpu.VMEM((all_tok, hid), F32),
            pltpu.VMEM((n_row, 16, hid), BF16),
            pltpu.VMEM((n_row, 16, hid), BF16),
            pltpu.VMEM((all_tok, hid), BF16),
            pltpu.VMEM((all_tok, feat), F32),
            pltpu.VMEM((feat, hid), BF16),
            pltpu.VMEM((ZHI, 5, tok, feat), BF16),
            pltpu.VMEM((ZHI, 5, tok, feat), BF16),
            pltpu.VMEM((ZHI, 2, tok, feat), BF16),
            pltpu.VMEM((ZHI, 2, tok, feat), BF16),
            pltpu.VMEM((ZHI, tok, feat), F32),
            pltpu.VMEM((ZHI, tok, feat), F32),
            dma((2,)),
            dma((ZHI,)),
            dma((ZHI,)),
            dma((ZHI, 7)),
            dma((ZHI, 7)),
            dma((n_row,)),
            dma((n_row,)),
            dma((n_row,)),
            dma((n_row,)),
            dma((ZHI, 7)),
            dma((ZHI, 7)),
            dma((ZHI,)),
            dma((ZHI,)),
        ],
        compiler_params=pltpu.CompilerParams(
            collective_id=0, has_side_effects=True, vmem_limit_bytes=32 * 1024 * 1024
        ),
    )(inputs, weight, hidden_bias, cotangent)


def solution(mesh):
    placed = (P("col", "row"), P("row", "col"), P("col"), P("row", "col"))
    return jax.shard_map(
        shards,
        mesh=mesh,
        in_specs=placed,
        out_specs=(P("row", "col"), P("col", "row"), P("row", "col"), P("col")),
        check_vma=False,
    )
```

```python
import jax
import jax.numpy as jnp
from jax import lax
from jax.experimental import pallas as pl
from jax.experimental.pallas import tpu as pltpu
from jax.sharding import PartitionSpec as P

MESH = pl.DeviceIdType.MESH
CORES, XS, ZLO, YS, ZHI = 2, 4, 2, 8, 4
ROWS, COLS = ZLO * XS * CORES, ZHI * YS
BF16, F32 = jnp.bfloat16, jnp.float32

ROW_OFFSETS = [
    (dz, dx, dc)
    for dz, dx in ((1, 2), (0, 2), (1, 1), (1, 3), (0, 1), (0, 3), (1, 0), (0, 0))
    for dc in (1, 0)
    if dz or dx or dc
]
CHIPS = [(1, 2), (1, 1), (1, 3), (0, 2), (1, 0), (0, 1), (0, 3)]
Z_ORDER = (0, 1, 3, 2)
FAR_SIDE = {0: 1, 1: -1, 3: 1, 2: -1}


def gelu_and_slope(v):
    c, a = 0.7978845608028654, 0.044715
    v2 = v * v
    t = jnp.tanh(c * (v + a * (v2 * v)))
    half = 0.5 * (1.0 + t)
    return v * half, half + (0.5 * v) * (1.0 - t * t) * (c * (1.0 + (3.0 * a) * v2))


def kernel(
    x_hbm, w_hbm, b_ref, cot_ref,
    hid_ref, gi_ref, gw_ref, gb_ref,
    w_v, xg, xn, xt, own, psend, precv, g_v, part2,
    raw, raw_in, mid, mid_in, zout, zin,
    local_sem, za_s, za_r, ya_s, ya_r, p_s, p_r, g_s, g_r, h_s, h_r, e_s, e_r, ez_s, ez_r,
):
    r = lax.axis_index("row")
    c = lax.axis_index("col")
    core, x, zlo = lax.rem(r, 2), lax.rem(lax.div(r, 2), XS), lax.div(r, 8)
    y, z = lax.rem(c, YS), lax.div(c, YS)

    def at_row(dz, dx, dc):
        return (lax.rem(zlo + dz, ZLO) * XS + lax.rem(x + dx, XS)) * CORES + lax.rem(core + dc, CORES)

    def wy(d):
        return lax.rem(y + (d + YS), YS)

    def wz(d):
        return lax.rem(z + (d + ZHI), ZHI)

    def to_row(o):
        return {"row": at_row(*o), "col": c}

    def to_y(d):
        return {"row": r, "col": z * YS + wy(d)}

    def to_z(d):
        return {"row": r, "col": wz(d) * YS + y}

    def send(src, dst, s, q, dev):
        return pltpu.make_async_remote_copy(
            src_ref=src, dst_ref=dst, send_sem=s, recv_sem=q, device_id=dev, device_id_type=MESH
        )

    peers = [to_y(d) for d in (1, -1, 2, -2)] + [to_z(d) for d in (1, 2, 3)] + [to_row(o) for o in ROW_OFFSETS]
    barrier = pltpu.get_barrier_semaphore()
    for dev in peers:
        pl.semaphore_signal(barrier, inc=1, device_id=dev, device_id_type=MESH)
    x_in = pltpu.make_async_copy(x_hbm, xg.at[y, z], local_sem.at[0])
    w_in = pltpu.make_async_copy(w_hbm, w_v, local_sem.at[1])
    x_in.start()
    w_in.start()
    x_in.wait()
    pl.semaphore_wait(barrier, len(peers))

    pending = []
    zc, near = {}, {}
    far = {k: [] for k in Z_ORDER}

    def forward_near(k):
        for i, d in enumerate((2, -2, 1, -1)):
            block = xg.at[y, wz(-k)]
            near[k, d] = send(block, block, ya_s.at[k, i], ya_r.at[k, i], to_y(d))
            near[k, d].start()
            pending.append(near[k, d])

    def forward_far(k):
        for i, side in enumerate((1, -1)):
            near[k, 2 * side].wait_recv()
            block = xg.at[wy(-2 * side), wz(-k)]
            if FAR_SIDE[k] == side:
                far[k].append(send(block, block, ya_s.at[k, 4], ya_r.at[k, 4], to_y(2 * side)))
                far[k][-1].start()
            far[k].append(send(block, block, ya_s.at[k, 5 + i], ya_r.at[k, 5 + i], to_y(side)))
            far[k][-1].start()
        pending.extend(far[k])

    def multiply(k):
        zk = wz(-k)
        for cp in [near[k, 1], near[k, -1]] + far[k]:
            cp.wait_recv()
        rows = pl.ds(pl.multiple_of(zk * 64, 64), 64)
        xs = jnp.concatenate([xg[yy, zk].astype(F32) for yy in range(YS)], axis=0).astype(BF16)
        xn[rows, :] = xs
        share = jnp.dot(xs, w_v[...], preferred_element_type=F32)
        for j in range(4):
            owner = zk * 4 + j
            d = lax.rem(owner - r + ROWS, ROWS)
            part = share[16 * j : 16 * j + 16, :]
            psend[4 * k + j] = part.astype(BF16)

            @pl.when(d != 0)
            def _():
                send(psend.at[4 * k + j], precv.at[d], p_s.at[d], p_r.at[d], {"row": owner, "col": c}).start()

            @pl.when(d == 0)
            def _():
                own[...] = part

    for d in (2, 1, 3):
        zc[d] = send(xg.at[y, z], xg.at[y, z], za_s.at[d], za_r.at[d], to_z(d))
        zc[d].start()
        pending.append(zc[d])
    forward_near(0)
    for k in (1, 3):
        zc[k].wait_recv()
        forward_near(k)
    forward_far(0)
    zc[2].wait_recv()
    forward_near(2)
    w_in.wait()
    forward_far(1)
    forward_far(3)
    multiply(0)
    forward_far(2)
    for k in (1, 3, 2):
        multiply(k)

    xt[...] = xn[...].T
    v = own[...] + b_ref[...].reshape(1, -1)
    for d in range(1, ROWS):
        cp = send(psend.at[d], precv.at[d], p_s.at[d], p_r.at[d], to_row(ROW_OFFSETS[0]))
        cp.wait_recv()
        pending.append(cp)
        v = v + precv[d].astype(F32)

    mine = pl.ds(pl.multiple_of(r * 16, 16), 16)
    hidden, slope = gelu_and_slope(v)
    g_v[mine, :] = (cot_ref[...].astype(F32) * slope).astype(BF16)

    other = {"row": at_row(0, 0, 1), "col": c}
    grads, passed = [], []
    for i, (dz, dx) in enumerate(CHIPS):
        grads.append(send(g_v.at[mine, :], g_v.at[mine, :], g_s.at[i], g_r.at[i], to_row((dz, dx, 0))))
        grads[-1].start()

    def hand_over(i, rows):
        passed.append(send(g_v.at[rows, :], g_v.at[rows, :], h_s.at[i], h_r.at[i], other))
        passed[-1].start()

    hand_over(len(CHIPS), mine)
    hid_ref[...] = hidden.astype(BF16)
    for i in reversed(range(len(CHIPS))):
        dz, dx = CHIPS[i]
        grads[i].wait_recv()
        hand_over(i, pl.ds(pl.multiple_of(at_row(ZLO - dz, XS - dx, 0) * 16, 16), 16))
    for cp in passed:
        cp.wait_recv()
    pending += grads + passed

    legs = {}

    def share(d, zk):
        return part2[pl.ds(pl.multiple_of((zk * YS + wy(d)) * 8, 8), 8), :]

    def leave(k, j, src, dst, d):
        legs[k, j] = send(src, dst, e_s.at[k, j], e_r.at[k, j], to_y(d))
        legs[k, j].start()
        pending.append(legs[k, j])

    def first_legs(k, which):
        zk = wz(k)
        for j, final, via in which:
            raw[k, j] = share(final, zk).astype(BF16)
            leave(k, j, raw.at[k, j], raw_in.at[k, j], via(k))

    def second_legs(k):
        zk = wz(k)
        legs[k, 0].wait_recv()
        for j, side in ((0, 1), (1, -1)):
            legs[k, 1 + j].wait_recv()
            s = share(2 * side, zk) + raw_in[k, 1 + j].astype(F32)
            if FAR_SIDE[k] == side:
                s = s + raw_in[k, 0].astype(F32)
            mid[k, j] = s.astype(BF16)
            leave(k, 5 + j, mid.at[k, j], mid_in.at[k, j], 2 * side)

    def y_total(k):
        s = share(0, wz(k))
        for j in (3, 4):
            legs[k, j].wait_recv()
            s = s + raw_in[k, j].astype(F32)
        for j in (0, 1):
            legs[k, 5 + j].wait_recv()
            s = s + mid_in[k, j].astype(F32)
        return s

    last = {}

    def z_leg(k):
        zout[k] = y_total(k).astype(BF16)
        last[k] = send(zout.at[k], zin.at[k], ez_s.at[k], ez_r.at[k], to_z(k))
        last[k].start()
        pending.append(last[k])

    part2[...] = lax.dot_general(g_v[...], w_v[...], (((1,), (1,)), ((), ())), preferred_element_type=F32)
    order = (2, 1, 3, 0)
    for k in order:
        first_legs(k, ((0, 4, lambda k: 2 * FAR_SIDE[k]), (1, 3, lambda k: 1), (2, -3, lambda k: -1)))
    for k in order:
        first_legs(k, ((3, 1, lambda k: 1), (4, -1, lambda k: -1)))
    gw_ref[...] = jnp.dot(xt[...], g_v[...], preferred_element_type=F32).astype(BF16)
    gb_ref[...] = jnp.sum(g_v[...].astype(F32), axis=0)
    for k in order:
        second_legs(k)
    z_leg(2)
    z_leg(1)
    z_leg(3)
    s = y_total(0)
    for k in (1, 3, 2):
        last[k].wait_recv()
        s = s + zin[k].astype(F32)
    gi_ref[...] = s.astype(BF16)
    for cp in pending:
        cp.wait_send()


def store(*refs):
    sem = refs[8]
    copies = [pltpu.make_async_copy(refs[i], refs[4 + i], sem.at[i]) for i in range(4)]
    for cp in copies:
        cp.start()
    for cp in copies:
        cp.wait()


def shards(inputs, weight, hidden_bias, cotangent):
    tok, feat = inputs.shape
    hid = weight.shape[1]
    all_tok = tok * COLS
    vmem = pl.BlockSpec(memory_space=pltpu.VMEM)
    hbm = pl.BlockSpec(memory_space=pl.ANY)
    dma = pltpu.SemaphoreType.DMA
    outs = pl.pallas_call(
        kernel,
        out_shape=(
            pltpu.VMEM(cotangent.shape, BF16),
            pltpu.VMEM(inputs.shape, BF16),
            pltpu.VMEM(weight.shape, BF16),
            pltpu.VMEM(hidden_bias.shape, F32),
        ),
        in_specs=[hbm, hbm, vmem, vmem],
        out_specs=(vmem, vmem, vmem, vmem),
        scratch_shapes=[
            pltpu.VMEM((feat, hid), BF16),
            pltpu.VMEM((YS, ZHI, tok, feat), BF16),
            pltpu.VMEM((all_tok, feat), BF16),
            pltpu.VMEM((feat, all_tok), BF16),
            pltpu.VMEM((16, hid), F32),
            pltpu.VMEM((ROWS, 16, hid), BF16),
            pltpu.VMEM((ROWS, 16, hid), BF16),
            pltpu.VMEM((all_tok, hid), BF16),
            pltpu.VMEM((all_tok, feat), F32),
            pltpu.VMEM((ZHI, 5, tok, feat), BF16),
            pltpu.VMEM((ZHI, 5, tok, feat), BF16),
            pltpu.VMEM((ZHI, 2, tok, feat), BF16),
            pltpu.VMEM((ZHI, 2, tok, feat), BF16),
            pltpu.VMEM((ZHI, tok, feat), BF16),
            pltpu.VMEM((ZHI, tok, feat), BF16),
            dma((2,)),
            dma((ZHI,)),
            dma((ZHI,)),
            dma((ZHI, 7)),
            dma((ZHI, 7)),
            dma((ROWS,)),
            dma((ROWS,)),
            dma((len(CHIPS),)),
            dma((len(CHIPS),)),
            dma((len(CHIPS) + 1,)),
            dma((len(CHIPS) + 1,)),
            dma((ZHI, 7)),
            dma((ZHI, 7)),
            dma((ZHI,)),
            dma((ZHI,)),
        ],
        compiler_params=pltpu.CompilerParams(
            collective_id=0, has_side_effects=True, vmem_limit_bytes=32 * 1024 * 1024
        ),
    )(*(pltpu.with_memory_space_constraint(a, pltpu.HBM) for a in (inputs, weight, hidden_bias, cotangent)))
    return pl.pallas_call(
        store,
        out_shape=[pltpu.HBM(o.shape, o.dtype) for o in outs],
        in_specs=[vmem] * 4,
        out_specs=[hbm] * 4,
        scratch_shapes=[dma((4,))],
    )(*(pltpu.with_memory_space_constraint(o, pltpu.VMEM) for o in outs))


def solution(mesh):
    placed = (P("col", "row"), P("row", "col"), P("col"), P("row", "col"))
    return jax.shard_map(
        shards,
        mesh=mesh,
        in_specs=placed,
        out_specs=(P("row", "col"), P("col", "row"), P("row", "col"), P("col")),
        check_vma=False,
    )
```

```python
import jax
import jax.numpy as jnp
from jax import lax
from jax.experimental import pallas as pl
from jax.experimental.pallas import tpu as pltpu
from jax.sharding import PartitionSpec as P

MESH = pl.DeviceIdType.MESH
CORES, XS, ZLO, YS, ZHI = 2, 4, 2, 8, 4
ROWS, COLS = ZLO * XS * CORES, ZHI * YS
BF16, F32 = jnp.bfloat16, jnp.float32

CHIPS = [(1, 2), (1, 1), (1, 3), (0, 2), (1, 0), (0, 1), (0, 3)]
NEAR, FAR = (2, -2, 1, -1), (4, 3, -3)
Z_OFFSETS = (2, 1, 3)


def gelu_and_slope(v):
    c, a = 0.7978845608028654, 0.044715
    v2 = v * v
    t = jnp.tanh(c * (v + a * (v2 * v)))
    half = 0.5 * (1.0 + t)
    return v * half, half + (0.5 * v) * (1.0 - t * t) * (c * (1.0 + (3.0 * a) * v2))


def kernel(
    x_hbm, w_hbm, b_ref, cot_ref,
    hid_ref, gi_ref, gw_ref, gb_ref,
    w_v, xg, xn, xt, mine_f, own, csend, crecv, psend, precv, g_v, part2,
    y1_out, y1_in, z1_out, z1_in, y2_out, y2_in, z2_out, z2_in,
    local_sem, a_s, a_r, c_s, c_r, p_s, p_r, g_s, g_r, h_s, h_r,
    y1_s, y1_r, z1_s, z1_r, y2_s, y2_r, z2_s, z2_r,
):
    r = lax.axis_index("row")
    c = lax.axis_index("col")
    core, x, zlo = lax.rem(r, 2), lax.rem(lax.div(r, 2), XS), lax.div(r, 8)
    y, z = lax.rem(c, YS), lax.div(c, YS)

    def at_row(dz, dx, dc):
        return (lax.rem(zlo + dz, ZLO) * XS + lax.rem(x + dx, XS)) * CORES + lax.rem(core + dc, CORES)

    def wy(d):
        return lax.rem(y + (d + YS), YS)

    def wz(d):
        return lax.rem(z + (d + ZHI), ZHI)

    def to_chip(dz, dx):
        return {"row": at_row(dz, dx, 0), "col": c}

    def to_y(d):
        return {"row": r, "col": z * YS + wy(d)}

    def to_z(d):
        return {"row": r, "col": wz(d) * YS + y}

    other = {"row": at_row(0, 0, 1), "col": c}
    pending = []

    def send(src, dst, s, q, dev):
        cp = pltpu.make_async_remote_copy(
            src_ref=src, dst_ref=dst, send_sem=s, recv_sem=q, device_id=dev, device_id_type=MESH
        )
        cp.start()
        pending.append(cp)
        return cp

    peers = [to_z(d) for d in Z_OFFSETS] + [to_y(d) for d in FAR + NEAR] + [to_chip(*o) for o in CHIPS] + [other]
    barrier = pltpu.get_barrier_semaphore()
    for dev in peers:
        pl.semaphore_signal(barrier, inc=1, device_id=dev, device_id_type=MESH)
    x_in = pltpu.make_async_copy(x_hbm, xg.at[y, z], local_sem.at[0])
    w_in = pltpu.make_async_copy(w_hbm, w_v, local_sem.at[1])
    x_in.start()
    w_in.start()
    x_in.wait()
    pl.semaphore_wait(barrier, len(peers))

    blocks = {}

    def pass_on(k, d, hop_k, hop_d):
        block = xg.at[wy(-d), wz(-k)]
        key = k + hop_k, d + hop_d
        at = key[0], key[1] % YS
        blocks[key] = send(block, block, a_s.at[at], a_r.at[at], to_z(hop_k) if hop_k else to_y(hop_d))

    for d in FAR:
        pass_on(0, 0, 0, d)
    for k in Z_OFFSETS:
        pass_on(0, 0, k, 0)
    for d in NEAR:
        pass_on(0, 0, 0, d)
    for k, d in ((1, 0), (3, 0), (0, 3), (0, -3), (2, 0), (0, 4)):
        blocks[k, d].wait_recv()
        if k:
            for hop in NEAR:
                pass_on(k, d, 0, hop)
        else:
            for hop in Z_OFFSETS:
                pass_on(k, d, hop, 0)

    halves = {}

    def multiply(k):
        zk = wz(-k)
        for d in NEAR + (FAR if k else ()):
            blocks[k, d].wait_recv()
        rows = pl.ds(pl.multiple_of(zk * 64, 64), 64)
        xs = jnp.concatenate([xg[yy, zk].astype(F32) for yy in range(YS)], axis=0).astype(BF16)
        xn[rows, :] = xs
        psend_f = jnp.dot(xs, w_v[...], preferred_element_type=F32)
        for j in range(2):
            for cc in range(2):
                part = psend_f[32 * j + 16 * cc : 32 * j + 16 * cc + 16, :]

                @pl.when(core == cc)
                def _():
                    own[k, j] = part

                @pl.when(core != cc)
                def _():
                    csend[k, j] = part

        halves[k] = send(csend.at[k], crecv.at[k], c_s.at[k], c_r.at[k], other)

    def to_owners(k):
        zk = wz(-k)
        halves[k].wait_recv()
        for j in range(2):
            chip = zk * 2 + j
            d = lax.rem(chip - lax.div(r, 2) + 8, 8)
            part = own[k, j] + crecv[k, j]
            psend[k, j] = part.astype(BF16)

            @pl.when(d != 0)
            def _():
                pltpu.make_async_remote_copy(
                    src_ref=psend.at[k, j], dst_ref=precv.at[d], send_sem=p_s.at[d], recv_sem=p_r.at[d],
                    device_id={"row": chip * 2 + core, "col": c}, device_id_type=MESH,
                ).start()

            @pl.when(d == 0)
            def _():
                mine_f[...] = part

    w_in.wait()
    multiply(0)
    to_owners(0)
    multiply(1)
    multiply(3)
    to_owners(1)
    to_owners(3)
    multiply(2)
    to_owners(2)

    xt[...] = xn[...].T
    v = mine_f[...] + b_ref[...].reshape(1, -1)
    for d in range(1, 8):
        cp = pltpu.make_async_remote_copy(
            src_ref=psend.at[d // 2, d % 2], dst_ref=precv.at[d], send_sem=p_s.at[d], recv_sem=p_r.at[d],
            device_id=other, device_id_type=MESH,
        )
        cp.wait_recv()
        pending.append(cp)
        v = v + precv[d].astype(F32)

    mine = pl.ds(pl.multiple_of(r * 16, 16), 16)
    hidden, slope = gelu_and_slope(v)
    g_v[mine, :] = (cot_ref[...].astype(F32) * slope).astype(BF16)

    grads, passed = [], []
    for i, (dz, dx) in enumerate(CHIPS):
        grads.append(send(g_v.at[mine, :], g_v.at[mine, :], g_s.at[i], g_r.at[i], to_chip(dz, dx)))

    def hand_over(i, rows):
        passed.append(send(g_v.at[rows, :], g_v.at[rows, :], h_s.at[i], h_r.at[i], other))

    hand_over(len(CHIPS), mine)
    hid_ref[...] = hidden.astype(BF16)
    for i in reversed(range(len(CHIPS))):
        dz, dx = CHIPS[i]
        grads[i].wait_recv()
        hand_over(i, pl.ds(pl.multiple_of(at_row(ZLO - dz, XS - dx, 0) * 16, 16), 16))
    for cp in passed:
        cp.wait_recv()

    part2[...] = lax.dot_general(g_v[...], w_v[...], (((1,), (1,)), ((), ())), preferred_element_type=F32)

    def share(k, d):
        return part2[pl.ds(pl.multiple_of((wz(k) * YS + wy(d)) * 8, 8), 8), :]

    z1, y1, z2, y2 = {}, {}, {}, {}
    for k in Z_OFFSETS:
        for i, d in enumerate(FAR):
            z1_out[k, i] = share(k, d).astype(BF16)
        z1[k] = send(z1_out.at[k], z1_in.at[k], z1_s.at[k], z1_r.at[k], to_z(k))
    for i, d in enumerate(NEAR):
        for k in range(ZHI):
            y1_out[i, k] = share(k, d).astype(BF16)
        y1[d] = send(y1_out.at[i], y1_in.at[i], y1_s.at[i], y1_r.at[i], to_y(d))

    gw_ref[...] = jnp.dot(xt[...], g_v[...], preferred_element_type=F32).astype(BF16)
    gb_ref[...] = jnp.sum(g_v[...].astype(F32), axis=0)

    for d in NEAR:
        y1[d].wait_recv()
    for k in Z_OFFSETS:
        s = share(k, 0)
        for i in range(len(NEAR)):
            s = s + y1_in[i, k].astype(F32)
        z2_out[k] = s.astype(BF16)
        z2[k] = send(z2_out.at[k], z2_in.at[k], z2_s.at[k], z2_r.at[k], to_z(k))
    for k in Z_OFFSETS:
        z1[k].wait_recv()
    for i, d in enumerate(FAR):
        s = share(0, d)
        for k in Z_OFFSETS:
            s = s + z1_in[k, i].astype(F32)
        y2_out[i] = s.astype(BF16)
        y2[d] = send(y2_out.at[i], y2_in.at[i], y2_s.at[i], y2_r.at[i], to_y(d))
    s = share(0, 0)
    for i in range(len(NEAR)):
        s = s + y1_in[i, 0].astype(F32)
    for k in (1, 3, 2):
        z2[k].wait_recv()
        s = s + z2_in[k].astype(F32)
    for i, d in reversed(list(enumerate(FAR))):
        y2[d].wait_recv()
        s = s + y2_in[i].astype(F32)
    gi_ref[...] = s.astype(BF16)
    for cp in pending:
        cp.wait_send()


def store(*refs):
    sem = refs[8]
    copies = [pltpu.make_async_copy(refs[i], refs[4 + i], sem.at[i]) for i in range(4)]
    for cp in copies:
        cp.start()
    for cp in copies:
        cp.wait()


def shards(inputs, weight, hidden_bias, cotangent):
    tok, feat = inputs.shape
    hid = weight.shape[1]
    all_tok = tok * COLS
    vmem = pl.BlockSpec(memory_space=pltpu.VMEM)
    hbm = pl.BlockSpec(memory_space=pl.ANY)
    dma = pltpu.SemaphoreType.DMA
    outs = pl.pallas_call(
        kernel,
        out_shape=(
            pltpu.VMEM(cotangent.shape, BF16),
            pltpu.VMEM(inputs.shape, BF16),
            pltpu.VMEM(weight.shape, BF16),
            pltpu.VMEM(hidden_bias.shape, F32),
        ),
        in_specs=[hbm, hbm, vmem, vmem],
        out_specs=(vmem, vmem, vmem, vmem),
        scratch_shapes=[
            pltpu.VMEM((feat, hid), BF16),
            pltpu.VMEM((YS, ZHI, tok, feat), BF16),
            pltpu.VMEM((all_tok, feat), BF16),
            pltpu.VMEM((feat, all_tok), BF16),
            pltpu.VMEM((16, hid), F32),
            pltpu.VMEM((ZHI, 2, 16, hid), F32),
            pltpu.VMEM((ZHI, 2, 16, hid), F32),
            pltpu.VMEM((ZHI, 2, 16, hid), F32),
            pltpu.VMEM((ZHI, 2, 16, hid), BF16),
            pltpu.VMEM((8, 16, hid), BF16),
            pltpu.VMEM((all_tok, hid), BF16),
            pltpu.VMEM((all_tok, feat), F32),
            pltpu.VMEM((4, ZHI, tok, feat), BF16),
            pltpu.VMEM((4, ZHI, tok, feat), BF16),
            pltpu.VMEM((ZHI, 3, tok, feat), BF16),
            pltpu.VMEM((ZHI, 3, tok, feat), BF16),
            pltpu.VMEM((3, tok, feat), BF16),
            pltpu.VMEM((3, tok, feat), BF16),
            pltpu.VMEM((ZHI, tok, feat), BF16),
            pltpu.VMEM((ZHI, tok, feat), BF16),
            dma((2,)),
            dma((ZHI, YS)),
            dma((ZHI, YS)),
            dma((ZHI,)),
            dma((ZHI,)),
            dma((8,)),
            dma((8,)),
            dma((len(CHIPS),)),
            dma((len(CHIPS),)),
            dma((len(CHIPS) + 1,)),
            dma((len(CHIPS) + 1,)),
            dma((4,)),
            dma((4,)),
            dma((ZHI,)),
            dma((ZHI,)),
            dma((3,)),
            dma((3,)),
            dma((ZHI,)),
            dma((ZHI,)),
        ],
        compiler_params=pltpu.CompilerParams(
            collective_id=0, has_side_effects=True, vmem_limit_bytes=32 * 1024 * 1024
        ),
    )(*(pltpu.with_memory_space_constraint(a, pltpu.HBM) for a in (inputs, weight, hidden_bias, cotangent)))
    return pl.pallas_call(
        store,
        out_shape=[pltpu.HBM(o.shape, o.dtype) for o in outs],
        in_specs=[vmem] * 4,
        out_specs=[hbm] * 4,
        scratch_shapes=[dma((4,))],
    )(*(pltpu.with_memory_space_constraint(o, pltpu.VMEM) for o in outs))


def solution(mesh):
    placed = (P("col", "row"), P("row", "col"), P("col"), P("row", "col"))
    return jax.shard_map(
        shards,
        mesh=mesh,
        in_specs=placed,
        out_specs=(P("row", "col"), P("col", "row"), P("row", "col"), P("col")),
        check_vma=False,
    )
```

```python
import jax
import jax.numpy as jnp
from jax import lax
from jax.experimental import pallas as pl
from jax.experimental.pallas import tpu as pltpu
from jax.sharding import PartitionSpec as P

MESH = pl.DeviceIdType.MESH
CORES, XS, ZLO, YS, ZHI = 2, 4, 2, 8, 4
ROWS, COLS = ZLO * XS * CORES, ZHI * YS
BF16, F32 = jnp.bfloat16, jnp.float32

CHIPS = [(1, 2), (1, 1), (1, 3), (0, 2), (1, 0), (0, 1), (0, 3)]
NEAR, FAR = (2, -2, 1, -1), (4, 3, -3)
Z_OFFSETS = (2, 1, 3)


def gelu_and_slope(v):
    c, a = 0.7978845608028654, 0.044715
    v2 = v * v
    t = jnp.tanh(c * (v + a * (v2 * v)))
    half = 0.5 * (1.0 + t)
    return v * half, half + (0.5 * v) * (1.0 - t * t) * (c * (1.0 + (3.0 * a) * v2))


def kernel(
    x_hbm, w_hbm, b_hbm, cot_hbm,
    hid_ref, gi_ref, gw_ref, gb_ref,
    w_v, b_v, cot_v, xg, xn, xt, mine_f, own, csend, crecv, psend, precv, g_v, part2,
    y1_out, y1_in, z1_out, z1_in, y2_out, y2_in, z2_out, z2_in,
    local_sem, a_s, a_r, c_s, c_r, p_s, p_r, g_s, g_r, h_s, h_r,
    y1_s, y1_r, z1_s, z1_r, y2_s, y2_r, z2_s, z2_r,
):
    r = lax.axis_index("row")
    c = lax.axis_index("col")
    core, x, zlo = lax.rem(r, 2), lax.rem(lax.div(r, 2), XS), lax.div(r, 8)
    y, z = lax.rem(c, YS), lax.div(c, YS)

    def at_row(dz, dx, dc):
        return (lax.rem(zlo + dz, ZLO) * XS + lax.rem(x + dx, XS)) * CORES + lax.rem(core + dc, CORES)

    def wy(d):
        return lax.rem(y + (d + YS), YS)

    def wz(d):
        return lax.rem(z + (d + ZHI), ZHI)

    def to_chip(dz, dx):
        return {"row": at_row(dz, dx, 0), "col": c}

    def to_y(d):
        return {"row": r, "col": z * YS + wy(d)}

    def to_z(d):
        return {"row": r, "col": wz(d) * YS + y}

    other = {"row": at_row(0, 0, 1), "col": c}
    pending = []

    def send(src, dst, s, q, dev):
        cp = pltpu.make_async_remote_copy(
            src_ref=src, dst_ref=dst, send_sem=s, recv_sem=q, device_id=dev, device_id_type=MESH
        )
        cp.start()
        pending.append(cp)
        return cp

    peers = [to_z(d) for d in Z_OFFSETS] + [to_y(d) for d in FAR + NEAR] + [to_chip(*o) for o in CHIPS] + [other]
    barrier = pltpu.get_barrier_semaphore()
    x_in = pltpu.make_async_copy(x_hbm, xg.at[y, z], local_sem.at[0])
    x_in.start()
    for dev in peers:
        pl.semaphore_signal(barrier, inc=1, device_id=dev, device_id_type=MESH)
    w_in = pltpu.make_async_copy(w_hbm, w_v, local_sem.at[1])
    b_in = pltpu.make_async_copy(b_hbm, b_v, local_sem.at[2])
    cot_in = pltpu.make_async_copy(cot_hbm, cot_v, local_sem.at[3])
    for cp in (w_in, b_in, cot_in):
        cp.start()
    x_in.wait()
    pl.semaphore_wait(barrier, len(peers))

    blocks = {}

    def pass_on(k, d, hop_k, hop_d):
        block = xg.at[wy(-d), wz(-k)]
        key = k + hop_k, d + hop_d
        at = key[0], key[1] % YS
        blocks[key] = send(block, block, a_s.at[at], a_r.at[at], to_z(hop_k) if hop_k else to_y(hop_d))

    for d in FAR:
        pass_on(0, 0, 0, d)
    for k in Z_OFFSETS:
        pass_on(0, 0, k, 0)
    for d in NEAR:
        pass_on(0, 0, 0, d)
    for k, d in ((1, 0), (3, 0), (0, 3), (0, -3), (2, 0), (0, 4)):
        blocks[k, d].wait_recv()
        if k:
            for hop in NEAR:
                pass_on(k, d, 0, hop)
        else:
            for hop in Z_OFFSETS:
                pass_on(k, d, hop, 0)

    halves = {}

    def multiply(k):
        zk = wz(-k)
        for d in NEAR + (FAR if k else ()):
            blocks[k, d].wait_recv()
        rows = pl.ds(pl.multiple_of(zk * 64, 64), 64)
        xs = jnp.concatenate([xg[yy, zk].astype(F32) for yy in range(YS)], axis=0).astype(BF16)
        xn[rows, :] = xs
        psend_f = jnp.dot(xs, w_v[...], preferred_element_type=F32)
        for j in range(2):
            for cc in range(2):
                part = psend_f[32 * j + 16 * cc : 32 * j + 16 * cc + 16, :]

                @pl.when(core == cc)
                def _():
                    own[k, j] = part

                @pl.when(core != cc)
                def _():
                    csend[k, j] = part

        halves[k] = send(csend.at[k], crecv.at[k], c_s.at[k], c_r.at[k], other)

    def to_owners(k):
        zk = wz(-k)
        halves[k].wait_recv()
        for j in range(2):
            chip = zk * 2 + j
            d = lax.rem(chip - lax.div(r, 2) + 8, 8)
            part = own[k, j] + crecv[k, j]
            psend[k, j] = part.astype(BF16)

            @pl.when(d != 0)
            def _():
                pltpu.make_async_remote_copy(
                    src_ref=psend.at[k, j], dst_ref=precv.at[d], send_sem=p_s.at[d], recv_sem=p_r.at[d],
                    device_id={"row": chip * 2 + core, "col": c}, device_id_type=MESH,
                ).start()

            @pl.when(d == 0)
            def _():
                mine_f[...] = part

    for cp in (w_in, b_in, cot_in):
        cp.wait()
    multiply(0)
    to_owners(0)
    multiply(1)
    multiply(3)
    to_owners(1)
    to_owners(3)
    multiply(2)
    to_owners(2)

    xt[...] = xn[...].T
    v = mine_f[...] + b_v[...].reshape(1, -1)
    for d in range(1, 8):
        cp = pltpu.make_async_remote_copy(
            src_ref=psend.at[d // 2, d % 2], dst_ref=precv.at[d], send_sem=p_s.at[d], recv_sem=p_r.at[d],
            device_id=other, device_id_type=MESH,
        )
        cp.wait_recv()
        pending.append(cp)
        v = v + precv[d].astype(F32)

    mine = pl.ds(pl.multiple_of(r * 16, 16), 16)
    hidden, slope = gelu_and_slope(v)
    g_v[mine, :] = (cot_v[...].astype(F32) * slope).astype(BF16)

    grads, passed = [], []
    for i, (dz, dx) in enumerate(CHIPS):
        grads.append(send(g_v.at[mine, :], g_v.at[mine, :], g_s.at[i], g_r.at[i], to_chip(dz, dx)))

    def hand_over(i, rows):
        passed.append(send(g_v.at[rows, :], g_v.at[rows, :], h_s.at[i], h_r.at[i], other))

    hand_over(len(CHIPS), mine)
    hid_ref[...] = hidden.astype(BF16)
    for i in reversed(range(len(CHIPS))):
        dz, dx = CHIPS[i]
        grads[i].wait_recv()
        hand_over(i, pl.ds(pl.multiple_of(at_row(ZLO - dz, XS - dx, 0) * 16, 16), 16))
    for cp in passed:
        cp.wait_recv()

    part2[...] = lax.dot_general(g_v[...], w_v[...], (((1,), (1,)), ((), ())), preferred_element_type=F32)

    def share(k, d):
        return part2[pl.ds(pl.multiple_of((wz(k) * YS + wy(d)) * 8, 8), 8), :]

    z1, y1, z2, y2 = {}, {}, {}, {}
    for k in Z_OFFSETS:
        for i, d in enumerate(FAR):
            z1_out[k, i] = share(k, d).astype(BF16)
        z1[k] = send(z1_out.at[k], z1_in.at[k], z1_s.at[k], z1_r.at[k], to_z(k))
    for i, d in enumerate(NEAR):
        for k in range(ZHI):
            y1_out[i, k] = share(k, d).astype(BF16)
        y1[d] = send(y1_out.at[i], y1_in.at[i], y1_s.at[i], y1_r.at[i], to_y(d))

    gw_ref[...] = jnp.dot(xt[...], g_v[...], preferred_element_type=F32).astype(BF16)
    gb_ref[...] = jnp.sum(g_v[...].astype(F32), axis=0)

    for k in Z_OFFSETS:
        z1[k].wait_recv()
    for i, d in enumerate(FAR):
        s = share(0, d)
        for k in Z_OFFSETS:
            s = s + z1_in[k, i].astype(F32)
        y2_out[i] = s.astype(BF16)
        y2[d] = send(y2_out.at[i], y2_in.at[i], y2_s.at[i], y2_r.at[i], to_y(d))
    for d in NEAR:
        y1[d].wait_recv()
    for k in Z_OFFSETS:
        s = share(k, 0)
        for i in range(len(NEAR)):
            s = s + y1_in[i, k].astype(F32)
        z2_out[k] = s.astype(BF16)
        z2[k] = send(z2_out.at[k], z2_in.at[k], z2_s.at[k], z2_r.at[k], to_z(k))
    s = share(0, 0)
    for i in range(len(NEAR)):
        s = s + y1_in[i, 0].astype(F32)
    for k in (1, 3, 2):
        z2[k].wait_recv()
        s = s + z2_in[k].astype(F32)
    for i, d in reversed(list(enumerate(FAR))):
        y2[d].wait_recv()
        s = s + y2_in[i].astype(F32)
    gi_ref[...] = s.astype(BF16)
    for cp in pending:
        cp.wait_send()


def store(*refs):
    sem = refs[8]
    copies = [pltpu.make_async_copy(refs[i], refs[4 + i], sem.at[i]) for i in range(4)]
    for cp in copies:
        cp.start()
    for cp in copies:
        cp.wait()


def shards(inputs, weight, hidden_bias, cotangent):
    tok, feat = inputs.shape
    hid = weight.shape[1]
    all_tok = tok * COLS
    vmem = pl.BlockSpec(memory_space=pltpu.VMEM)
    hbm = pl.BlockSpec(memory_space=pl.ANY)
    dma = pltpu.SemaphoreType.DMA
    outs = pl.pallas_call(
        kernel,
        out_shape=(
            pltpu.VMEM(cotangent.shape, BF16),
            pltpu.VMEM(inputs.shape, BF16),
            pltpu.VMEM(weight.shape, BF16),
            pltpu.VMEM(hidden_bias.shape, F32),
        ),
        in_specs=[hbm] * 4,
        out_specs=(vmem, vmem, vmem, vmem),
        scratch_shapes=[
            pltpu.VMEM((feat, hid), BF16),
            pltpu.VMEM((hid,), F32),
            pltpu.VMEM((all_tok // ROWS, hid), BF16),
            pltpu.VMEM((YS, ZHI, tok, feat), BF16),
            pltpu.VMEM((all_tok, feat), BF16),
            pltpu.VMEM((feat, all_tok), BF16),
            pltpu.VMEM((16, hid), F32),
            pltpu.VMEM((ZHI, 2, 16, hid), F32),
            pltpu.VMEM((ZHI, 2, 16, hid), F32),
            pltpu.VMEM((ZHI, 2, 16, hid), F32),
            pltpu.VMEM((ZHI, 2, 16, hid), BF16),
            pltpu.VMEM((8, 16, hid), BF16),
            pltpu.VMEM((all_tok, hid), BF16),
            pltpu.VMEM((all_tok, feat), F32),
            pltpu.VMEM((4, ZHI, tok, feat), BF16),
            pltpu.VMEM((4, ZHI, tok, feat), BF16),
            pltpu.VMEM((ZHI, 3, tok, feat), BF16),
            pltpu.VMEM((ZHI, 3, tok, feat), BF16),
            pltpu.VMEM((3, tok, feat), BF16),
            pltpu.VMEM((3, tok, feat), BF16),
            pltpu.VMEM((ZHI, tok, feat), BF16),
            pltpu.VMEM((ZHI, tok, feat), BF16),
            dma((4,)),
            dma((ZHI, YS)),
            dma((ZHI, YS)),
            dma((ZHI,)),
            dma((ZHI,)),
            dma((8,)),
            dma((8,)),
            dma((len(CHIPS),)),
            dma((len(CHIPS),)),
            dma((len(CHIPS) + 1,)),
            dma((len(CHIPS) + 1,)),
            dma((4,)),
            dma((4,)),
            dma((ZHI,)),
            dma((ZHI,)),
            dma((3,)),
            dma((3,)),
            dma((ZHI,)),
            dma((ZHI,)),
        ],
        compiler_params=pltpu.CompilerParams(
            collective_id=0, has_side_effects=True, vmem_limit_bytes=32 * 1024 * 1024
        ),
    )(*(pltpu.with_memory_space_constraint(a, pltpu.HBM) for a in (inputs, weight, hidden_bias, cotangent)))
    return pl.pallas_call(
        store,
        out_shape=[pltpu.HBM(o.shape, o.dtype) for o in outs],
        in_specs=[vmem] * 4,
        out_specs=[hbm] * 4,
        scratch_shapes=[dma((4,))],
    )(*(pltpu.with_memory_space_constraint(o, pltpu.VMEM) for o in outs))


def solution(mesh):
    placed = (P("col", "row"), P("row", "col"), P("col"), P("row", "col"))
    return jax.shard_map(
        shards,
        mesh=mesh,
        in_specs=placed,
        out_specs=(P("row", "col"), P("col", "row"), P("row", "col"), P("col")),
        check_vma=False,
    )
```

```python
import jax
import jax.numpy as jnp
from jax import lax
from jax.experimental import pallas as pl
from jax.experimental.pallas import tpu as pltpu
from jax.sharding import PartitionSpec as P

MESH = pl.DeviceIdType.MESH
CORES, XS, ZLO, YS, ZHI = 2, 4, 2, 8, 4
ROWS, COLS = ZLO * XS * CORES, ZHI * YS
BF16, F32 = jnp.bfloat16, jnp.float32

CHIPS = [(1, 2), (1, 1), (1, 3), (0, 2), (1, 0), (0, 1), (0, 3)]
NEAR, FAR = (2, -2, 1, -1), (4, 3, -3)
Z_OFFSETS = (2, 1, 3)


def gelu_and_slope(v):
    c, a = 0.7978845608028654, 0.044715
    v2 = v * v
    t = jnp.tanh(c * (v + a * (v2 * v)))
    half = 0.5 * (1.0 + t)
    return v * half, half + (0.5 * v) * (1.0 - t * t) * (c * (1.0 + (3.0 * a) * v2))


def kernel(
    x_hbm, w_hbm, b_hbm, cot_hbm,
    hid_ref, gi_ref, gw_ref, gb_ref,
    w_v, b_v, cot_v, xg, xn, xt, mine_f, own, csend, crecv, psend, precv, g_v, part2,
    y1_out, y1_in, z1_out, z1_in, y2_out, y2_in, z2_out, z2_in,
    local_sem, a_s, a_r, c_s, c_r, p_s, p_r, g_s, g_r, h_s, h_r,
    y1_s, y1_r, z1_s, z1_r, y2_s, y2_r, z2_s, z2_r,
):
    r = lax.axis_index("row")
    c = lax.axis_index("col")
    core, x, zlo = lax.rem(r, 2), lax.rem(lax.div(r, 2), XS), lax.div(r, 8)
    y, z = lax.rem(c, YS), lax.div(c, YS)

    def at_row(dz, dx, dc):
        return (lax.rem(zlo + dz, ZLO) * XS + lax.rem(x + dx, XS)) * CORES + lax.rem(core + dc, CORES)

    def wy(d):
        return lax.rem(y + (d + YS), YS)

    def wz(d):
        return lax.rem(z + (d + ZHI), ZHI)

    def to_chip(dz, dx):
        return {"row": at_row(dz, dx, 0), "col": c}

    def to_y(d):
        return {"row": r, "col": z * YS + wy(d)}

    def to_z(d):
        return {"row": r, "col": wz(d) * YS + y}

    other = {"row": at_row(0, 0, 1), "col": c}
    pending = []

    def send(src, dst, s, q, dev):
        cp = pltpu.make_async_remote_copy(
            src_ref=src, dst_ref=dst, send_sem=s, recv_sem=q, device_id=dev, device_id_type=MESH
        )
        cp.start()
        pending.append(cp)
        return cp

    peers = [to_z(d) for d in Z_OFFSETS] + [to_y(d) for d in FAR + NEAR] + [to_chip(*o) for o in CHIPS] + [other]
    barrier = pltpu.get_barrier_semaphore()
    x_in = pltpu.make_async_copy(x_hbm, xg.at[y, z], local_sem.at[0])
    x_in.start()
    for dev in peers:
        pl.semaphore_signal(barrier, inc=1, device_id=dev, device_id_type=MESH)
    w_in = pltpu.make_async_copy(w_hbm, w_v, local_sem.at[1])
    b_in = pltpu.make_async_copy(b_hbm, b_v, local_sem.at[2])
    cot_in = pltpu.make_async_copy(cot_hbm, cot_v, local_sem.at[3])
    for cp in (w_in, b_in, cot_in):
        cp.start()
    x_in.wait()
    pl.semaphore_wait(barrier, len(peers))

    blocks = {}

    def pass_on(k, d, hop_k, hop_d):
        block = xg.at[wy(-d), wz(-k)]
        key = k + hop_k, d + hop_d
        at = key[0], key[1] % YS
        blocks[key] = send(block, block, a_s.at[at], a_r.at[at], to_z(hop_k) if hop_k else to_y(hop_d))

    for d in FAR:
        pass_on(0, 0, 0, d)
    for k in Z_OFFSETS:
        pass_on(0, 0, k, 0)
    for d in NEAR:
        pass_on(0, 0, 0, d)
    for k, d in ((1, 0), (3, 0), (0, 3), (0, -3), (2, 0), (0, 4)):
        blocks[k, d].wait_recv()
        if k:
            for hop in NEAR:
                pass_on(k, d, 0, hop)
        else:
            for hop in Z_OFFSETS:
                pass_on(k, d, hop, 0)

    halves = {}

    def multiply(k):
        zk = wz(-k)
        for d in NEAR + (FAR if k else ()):
            blocks[k, d].wait_recv()
        rows = pl.ds(pl.multiple_of(zk * 64, 64), 64)
        xs = jnp.concatenate([xg[yy, zk].astype(F32) for yy in range(YS)], axis=0).astype(BF16)
        xn[rows, :] = xs
        psend_f = jnp.dot(xs, w_v[...], preferred_element_type=F32)
        for j in range(2):
            for cc in range(2):
                part = psend_f[32 * j + 16 * cc : 32 * j + 16 * cc + 16, :]

                @pl.when(core == cc)
                def _():
                    own[k, j] = part

                @pl.when(core != cc)
                def _():
                    csend[k, j] = part

        halves[k] = send(csend.at[k], crecv.at[k], c_s.at[k], c_r.at[k], other)

    def to_owners(k):
        zk = wz(-k)
        halves[k].wait_recv()
        for j in range(2):
            chip = zk * 2 + j
            d = lax.rem(chip - lax.div(r, 2) + 8, 8)
            part = own[k, j] + crecv[k, j]
            psend[k, j] = part.astype(BF16)

            @pl.when(d != 0)
            def _():
                pltpu.make_async_remote_copy(
                    src_ref=psend.at[k, j], dst_ref=precv.at[d], send_sem=p_s.at[d], recv_sem=p_r.at[d],
                    device_id={"row": chip * 2 + core, "col": c}, device_id_type=MESH,
                ).start()

            @pl.when(d == 0)
            def _():
                mine_f[...] = part

    for cp in (w_in, b_in, cot_in):
        cp.wait()
    multiply(0)
    to_owners(0)
    multiply(1)
    multiply(3)
    multiply(2)
    to_owners(1)
    to_owners(3)
    to_owners(2)

    xt[...] = xn[...].T
    v = mine_f[...] + b_v[...].reshape(1, -1)
    for d in range(1, 8):
        cp = pltpu.make_async_remote_copy(
            src_ref=psend.at[d // 2, d % 2], dst_ref=precv.at[d], send_sem=p_s.at[d], recv_sem=p_r.at[d],
            device_id=other, device_id_type=MESH,
        )
        cp.wait_recv()
        pending.append(cp)
        v = v + precv[d].astype(F32)

    mine = pl.ds(pl.multiple_of(r * 16, 16), 16)
    hidden, slope = gelu_and_slope(v)
    g_v[mine, :] = (cot_v[...].astype(F32) * slope).astype(BF16)

    grads, passed = [], []
    for i, (dz, dx) in enumerate(CHIPS):
        grads.append(send(g_v.at[mine, :], g_v.at[mine, :], g_s.at[i], g_r.at[i], to_chip(dz, dx)))

    def hand_over(i, rows):
        passed.append(send(g_v.at[rows, :], g_v.at[rows, :], h_s.at[i], h_r.at[i], other))

    hand_over(len(CHIPS), mine)
    hid_ref[...] = hidden.astype(BF16)
    for i in reversed(range(len(CHIPS))):
        dz, dx = CHIPS[i]
        grads[i].wait_recv()
        hand_over(i, pl.ds(pl.multiple_of(at_row(ZLO - dz, XS - dx, 0) * 16, 16), 16))
    for cp in passed:
        cp.wait_recv()

    part2[...] = lax.dot_general(g_v[...], w_v[...], (((1,), (1,)), ((), ())), preferred_element_type=F32)

    def share(k, d):
        return part2[pl.ds(pl.multiple_of((wz(k) * YS + wy(d)) * 8, 8), 8), :]

    z1, y1, z2, y2 = {}, {}, {}, {}
    for k in Z_OFFSETS:
        for i, d in enumerate(FAR):
            z1_out[k, i] = share(k, d).astype(BF16)
        z1[k] = send(z1_out.at[k], z1_in.at[k], z1_s.at[k], z1_r.at[k], to_z(k))
    for i, d in enumerate(NEAR):
        for k in range(ZHI):
            y1_out[i, k] = share(k, d).astype(BF16)
        y1[d] = send(y1_out.at[i], y1_in.at[i], y1_s.at[i], y1_r.at[i], to_y(d))

    gw_ref[...] = jnp.dot(xt[...], g_v[...], preferred_element_type=F32).astype(BF16)
    gb_ref[...] = jnp.sum(g_v[...].astype(F32), axis=0)

    for k in Z_OFFSETS:
        z1[k].wait_recv()
    for i, d in enumerate(FAR):
        s = share(0, d)
        for k in Z_OFFSETS:
            s = s + z1_in[k, i].astype(F32)
        y2_out[i] = s.astype(BF16)
        y2[d] = send(y2_out.at[i], y2_in.at[i], y2_s.at[i], y2_r.at[i], to_y(d))
    for d in NEAR:
        y1[d].wait_recv()
    for k in Z_OFFSETS:
        s = share(k, 0)
        for i in range(len(NEAR)):
            s = s + y1_in[i, k].astype(F32)
        z2_out[k] = s.astype(BF16)
        z2[k] = send(z2_out.at[k], z2_in.at[k], z2_s.at[k], z2_r.at[k], to_z(k))
    s = share(0, 0)
    for i in range(len(NEAR)):
        s = s + y1_in[i, 0].astype(F32)
    for k in (1, 3, 2):
        z2[k].wait_recv()
        s = s + z2_in[k].astype(F32)
    for i, d in reversed(list(enumerate(FAR))):
        y2[d].wait_recv()
        s = s + y2_in[i].astype(F32)
    gi_ref[...] = s.astype(BF16)
    for cp in pending:
        cp.wait_send()


def store(*refs):
    sem = refs[8]
    copies = [pltpu.make_async_copy(refs[i], refs[4 + i], sem.at[i]) for i in range(4)]
    for cp in copies:
        cp.start()
    for cp in copies:
        cp.wait()


def shards(inputs, weight, hidden_bias, cotangent):
    tok, feat = inputs.shape
    hid = weight.shape[1]
    all_tok = tok * COLS
    vmem = pl.BlockSpec(memory_space=pltpu.VMEM)
    hbm = pl.BlockSpec(memory_space=pl.ANY)
    dma = pltpu.SemaphoreType.DMA
    outs = pl.pallas_call(
        kernel,
        out_shape=(
            pltpu.VMEM(cotangent.shape, BF16),
            pltpu.VMEM(inputs.shape, BF16),
            pltpu.VMEM(weight.shape, BF16),
            pltpu.VMEM(hidden_bias.shape, F32),
        ),
        in_specs=[hbm] * 4,
        out_specs=(vmem, vmem, vmem, vmem),
        scratch_shapes=[
            pltpu.VMEM((feat, hid), BF16),
            pltpu.VMEM((hid,), F32),
            pltpu.VMEM((all_tok // ROWS, hid), BF16),
            pltpu.VMEM((YS, ZHI, tok, feat), BF16),
            pltpu.VMEM((all_tok, feat), BF16),
            pltpu.VMEM((feat, all_tok), BF16),
            pltpu.VMEM((16, hid), F32),
            pltpu.VMEM((ZHI, 2, 16, hid), F32),
            pltpu.VMEM((ZHI, 2, 16, hid), F32),
            pltpu.VMEM((ZHI, 2, 16, hid), F32),
            pltpu.VMEM((ZHI, 2, 16, hid), BF16),
            pltpu.VMEM((8, 16, hid), BF16),
            pltpu.VMEM((all_tok, hid), BF16),
            pltpu.VMEM((all_tok, feat), F32),
            pltpu.VMEM((4, ZHI, tok, feat), BF16),
            pltpu.VMEM((4, ZHI, tok, feat), BF16),
            pltpu.VMEM((ZHI, 3, tok, feat), BF16),
            pltpu.VMEM((ZHI, 3, tok, feat), BF16),
            pltpu.VMEM((3, tok, feat), BF16),
            pltpu.VMEM((3, tok, feat), BF16),
            pltpu.VMEM((ZHI, tok, feat), BF16),
            pltpu.VMEM((ZHI, tok, feat), BF16),
            dma((4,)),
            dma((ZHI, YS)),
            dma((ZHI, YS)),
            dma((ZHI,)),
            dma((ZHI,)),
            dma((8,)),
            dma((8,)),
            dma((len(CHIPS),)),
            dma((len(CHIPS),)),
            dma((len(CHIPS) + 1,)),
            dma((len(CHIPS) + 1,)),
            dma((4,)),
            dma((4,)),
            dma((ZHI,)),
            dma((ZHI,)),
            dma((3,)),
            dma((3,)),
            dma((ZHI,)),
            dma((ZHI,)),
        ],
        compiler_params=pltpu.CompilerParams(
            collective_id=0, has_side_effects=True, vmem_limit_bytes=32 * 1024 * 1024
        ),
    )(*(pltpu.with_memory_space_constraint(a, pltpu.HBM) for a in (inputs, weight, hidden_bias, cotangent)))
    return pl.pallas_call(
        store,
        out_shape=[pltpu.HBM(o.shape, o.dtype) for o in outs],
        in_specs=[vmem] * 4,
        out_specs=[hbm] * 4,
        scratch_shapes=[dma((4,))],
    )(*(pltpu.with_memory_space_constraint(o, pltpu.VMEM) for o in outs))


def solution(mesh):
    placed = (P("col", "row"), P("row", "col"), P("col"), P("row", "col"))
    return jax.shard_map(
        shards,
        mesh=mesh,
        in_specs=placed,
        out_specs=(P("row", "col"), P("col", "row"), P("row", "col"), P("col")),
        check_vma=False,
    )
```
